512 devices in a mesh: node: 16 (over z), tm: 32 (over y, x, core).
Axes of the slice: x: 4, y: 4, z: 16, core: 2. Of those that a mesh axis runs over, the one named last changes fastest.
Arguments:
- series: bfloat16 [4096, 16384], P('node', 'tm'), may hold values from -6 to 6
- conv_weight: bfloat16 [128, 128], replicated, may hold values from -0.5 to 0.5
- conv_bias: float32 [128], replicated, may hold values from -3 to 3
- mix_weight: bfloat16 [128, 64], replicated, may hold values from -0.75 to 0.75
- local_blocks: int32 [32, 2], P('node'), may hold values from 0 to 1
- local_values: bfloat16 [32, 2, 128, 128], P('node'), may hold values from -0.375 to 0.375
- send_rows: int32 [16, 16, 16], P('node'), may hold values from 0 to 255
- send_count: int32 [16, 16], replicated, may hold values from 0 to 16, as said below
- remote_values: bfloat16 [4096, 256], P('node'), may hold values from -1.5 to 1.5
- cotangent: bfloat16 [4096, 16384], P('node', 'tm'), may hold values from -6 to 6
Outputs:
- mixed_out: bfloat16 [4096, 16384], P('node', 'tm')
- input_grad: bfloat16 [4096, 16384], P('node', 'tm')
The draws below stay inside these ranges and needn't reach their ends.
Inputs may be any that keep to these rules, and one draw needn't show every extreme that they name: `local_blocks`: tile index within the same group. `send_rows`: row index within the sending group. `send_count`: in every draw some group receives 16 live slots from every group.
All inputs are finite; a program needn't handle non-finite values.
Results may differ from the reference program's by a relative error of at most 0.009.
Values may be sent and summed in bfloat16 or wider, within the bound.
No kernel may reach another device: no remote copies, remote signals or barrier semaphores. Data moves between devices by JAX's collectives and lax.ppermute only.
A program may use at most 64 MiB of HBM per device.

```python
import jax
import jax.numpy as jnp
from jax import lax

C = 64
TILE = 128
TILES_DEV = 2
LB = 2
CAP = 16
NODE_DEV = 256
GROUPS = 16
NODES = 4096
TIME = 256
DILATION_SIZE = 128
SLOTS = 256


def draw_send_count(key, part):
    key = jax.random.fold_in(key, 11)
    key_one, key_two, key_three = jax.random.split(key, 3)
    draw_one = jax.random.randint(key_one, (GROUPS, GROUPS), 0, CAP + 1)
    draw_two = jax.random.randint(key_two, (GROUPS, GROUPS), 0, CAP + 1)
    busiest = jax.random.randint(key_three, (), 0, GROUPS)
    column = jnp.arange(GROUPS)[None, :] == busiest
    return jnp.where(column, CAP, jnp.minimum(draw_one, draw_two)).astype(jnp.int32)


def with_ends(result, stream_key, smallest, high):
    shape = result.shape
    index_at = [jax.random.randint(jax.random.fold_in(stream_key, axis), (), 0, shape[axis]) for axis in range(len(shape))]
    result = result.at[tuple(index_at)].set(smallest)
    longest = shape.index(max(shape))
    index_at[longest] = (index_at[longest] + 1) % shape[longest]
    return result.at[tuple(index_at)].set(high)


def block_levels(key, shape, pieces, least, top_value):
    gain, own = 1.0, jax.random.fold_in(key, 6)
    for dim, parts in pieces:
        draws = jnp.exp(jax.random.uniform(jax.random.fold_in(own, dim), (parts,), jnp.float32, least / len(pieces), top_value / len(pieces)))
        gain = gain * jnp.repeat(draws, shape[dim] // parts).reshape([-1 if axis == dim else 1 for axis in range(len(shape))])
    return gain


def normal_values(rng, extent, deviation, reach, cuts=(), kind=jnp.bfloat16):
    result = jax.random.normal(rng, extent, jnp.float32) * deviation
    if len(cuts) > 0:
        result = block_levels(rng, extent, cuts, -0.22, 0.18) * result
    return jnp.clip(result, min=-reach, max=reach).astype(kind)


def setup_inputs(seed: int = 0) -> dict:
    keys = jax.random.split(jax.random.key(seed), 11)
    return {
        "series": normal_values(keys[0], (NODES, TIME * C), 1.0, 6.0, ((0, 16), (1, 32))),
        "conv_weight": normal_values(keys[1], (2 * C, 2 * C), (2 * C) ** -0.5, 0.5),
        "conv_bias": normal_values(keys[2], (2 * C,), 0.5, 3.0, (), jnp.float32),
        "mix_weight": normal_values(keys[3], (2 * C, C), C ** -0.5, 0.75),
        "local_blocks": with_ends(jax.random.randint(keys[4], (NODES // TILE, LB), 0, TILES_DEV), jax.random.fold_in(keys[4], 1), 0, TILES_DEV - 1).astype(jnp.int32),
        "local_values": normal_values(keys[5], (NODES // TILE, LB, TILE, TILE), (LB * TILE) ** -0.5, 0.375, ((0, 16),)),
        "send_rows": with_ends(jax.random.randint(keys[6], (GROUPS, GROUPS, CAP), 0, NODE_DEV), jax.random.fold_in(keys[6], 1), 0, NODE_DEV - 1).astype(jnp.int32),
        "send_count": draw_send_count(jax.random.fold_in(keys[10], 71), 0),
        "remote_values": normal_values(keys[8], (NODES, SLOTS), CAP ** -0.5, 1.5, ((0, 16),)),
        "cotangent": normal_values(keys[9], (NODES, TIME * C), 1.0, 6.0, ((0, 16), (1, 32))),
    }


def gated_preact(rows_now, rows_before, conv_weight, conv_bias):
    stacked = jnp.concatenate([rows_before, rows_now], axis=1)
    return jnp.dot(stacked, conv_weight, preferred_element_type=jnp.float32) + conv_bias

def activate(preact, width):
    filtered = jnp.tanh(preact[:, :width])
    opened = jax.nn.sigmoid(preact[:, width:])
    return (filtered * opened).astype(jnp.bfloat16)

def gate_grad(upstream, preact, width):
    upstream = lax.optimization_barrier(upstream).astype(jnp.float32)
    filtered = jnp.tanh(preact[:, :width])
    opened = jax.nn.sigmoid(preact[:, width:])
    first_half = upstream * opened * (1.0 - filtered * filtered)
    second_half = upstream * filtered * opened * (1.0 - opened)
    return jnp.concatenate([first_half, second_half], axis=1).astype(jnp.bfloat16)

def lagged_steps(current_block, shift_len):
    zeros = jnp.zeros((current_block.shape[0], shift_len, current_block.shape[2]), current_block.dtype)
    return jnp.concatenate([zeros, current_block[:, :current_block.shape[1] - shift_len]], axis=1)

def forward_shift_steps(current_block, shift_len):
    zeros = jnp.zeros((current_block.shape[0], shift_len, current_block.shape[2]), current_block.dtype)
    return jnp.concatenate([current_block[:, shift_len:], zeros], axis=1)

def reference(series, conv_weight, conv_bias, mix_weight, local_blocks, local_values, send_rows, send_count, remote_values, cotangent):
    columns = TIME * C
    group_ids = jnp.arange(GROUPS, dtype=jnp.int32)

    def group_slice(array, index, length):
        return lax.dynamic_slice_in_dim(array, index * length, length, 0)

    def conv_group(index):
        current_block = group_slice(series, index, NODE_DEV).reshape(NODE_DEV, TIME, C)
        previous_values = lagged_steps(current_block, DILATION_SIZE)
        return gated_preact(current_block.reshape(-1, C), previous_values.reshape(-1, C), conv_weight, conv_bias)
    hidden = lax.map(lambda index: activate(conv_group(index), C).reshape(NODE_DEV, columns), group_ids)

    def remote_mask(index):
        counts_in = lax.dynamic_slice_in_dim(send_count, index, 1, 1)[:, 0]
        alive = (jnp.arange(CAP, dtype=jnp.int32)[None, :] < counts_in[:, None]).reshape(SLOTS)
        return group_slice(remote_values, index, NODE_DEV) * alive.astype(jnp.bfloat16)[None, :]

    def mixed_gradient(index):
        grad_rows = group_slice(cotangent, index, NODE_DEV).reshape(-1, C)
        grads = jnp.dot(grad_rows, mix_weight.T, preferred_element_type=jnp.float32)
        return (grads, grads[:, C:].astype(jnp.bfloat16).reshape(NODE_DEV, columns))

    def forward_group(index):
        own = hidden[index]
        tiled = own.reshape(TILES_DEV, TILE, columns)
        blocks = group_slice(local_blocks, index, TILES_DEV)
        values = group_slice(local_values, index, TILES_DEV)
        sources = tiled[blocks]
        local_sum = jnp.einsum('tbij,tbjc->tic', values.astype(jnp.float32), sources.astype(jnp.float32)).reshape(NODE_DEV, columns)
        rows_in = send_rows[:, index, :]
        gathered = hidden[group_ids[:, None], rows_in].reshape(SLOTS, columns)
        masked = remote_mask(index)
        remote_sum = jnp.dot(masked, gathered, preferred_element_type=jnp.float32)
        mixed = (local_sum + remote_sum).astype(jnp.bfloat16)
        both = jnp.concatenate([own.reshape(-1, C), mixed.reshape(-1, C)], axis=1)
        current = group_slice(series, index, NODE_DEV).reshape(-1, C)
        output = (current.astype(jnp.float32) + jnp.dot(both, mix_weight, preferred_element_type=jnp.float32)).astype(jnp.bfloat16)
        grads, mixed_grad = mixed_gradient(index)
        returned = jnp.dot(masked.T, mixed_grad, preferred_element_type=jnp.float32).astype(jnp.bfloat16)
        return (output.reshape(NODE_DEV, columns), returned)
    outputs, returned = lax.map(forward_group, group_ids)
    mixed_out = outputs.reshape(NODES, columns)

    def backward_group(index):
        grads, mixed_grad = mixed_gradient(index)
        blocks = group_slice(local_blocks, index, TILES_DEV)
        values = group_slice(local_values, index, TILES_DEV)
        tiled_grad = mixed_grad.reshape(TILES_DEV, TILE, columns)
        contrib = jnp.einsum('tbij,tic->tbjc', values.astype(jnp.float32), tiled_grad.astype(jnp.float32))
        selector = (blocks[None, :, :] == jnp.arange(TILES_DEV, dtype=jnp.int32)[:, None, None]).astype(jnp.float32)
        local_grad = jnp.einsum('ktb,tbjc->kjc', selector, contrib).reshape(NODE_DEV, columns)
        back_rows = lax.dynamic_slice_in_dim(returned, index * CAP, CAP, 1).reshape(SLOTS, columns)
        own_rows = send_rows[index].reshape(SLOTS)
        picker = (jnp.arange(NODE_DEV, dtype=jnp.int32)[:, None] == own_rows[None, :]).astype(jnp.bfloat16)
        remote_grad = jnp.dot(picker, back_rows, preferred_element_type=jnp.float32)
        hidden_grad = (grads[:, :C].reshape(NODE_DEV, columns) + local_grad + remote_grad).astype(jnp.bfloat16)
        preact = conv_group(index)
        gate_out = gate_grad(hidden_grad.reshape(-1, C), preact, C)
        conv_back = jnp.dot(gate_out, conv_weight.T, preferred_element_type=jnp.float32)
        previous_gradient = lax.optimization_barrier(conv_back[:, :C].astype(jnp.bfloat16)).reshape(NODE_DEV, TIME, C)
        future_values = forward_shift_steps(previous_gradient, DILATION_SIZE)
        conv_grad = (conv_back[:, C:].reshape(NODE_DEV, TIME, C) + future_values.astype(jnp.float32)).astype(jnp.bfloat16)
        conv_grad = lax.optimization_barrier(conv_grad).reshape(NODE_DEV, columns)
        grad_block = group_slice(cotangent, index, NODE_DEV)
        return (grad_block.astype(jnp.float32) + conv_grad.astype(jnp.float32)).astype(jnp.bfloat16)
    input_grad = lax.map(backward_group, group_ids).reshape(NODES, columns)
    return (mixed_out, input_grad)
```

```python
import jax
import jax.numpy as jnp
from jax import lax
from jax.experimental import pallas as pl
from jax.experimental.pallas import tpu as pltpu
from jax.sharding import PartitionSpec as P

C = 64
PAIR = 2 * C
F32 = jnp.float32
BF16 = jnp.bfloat16


def dot(a, b):
    return lax.dot_general(a, b, (((1,), (0,)), ((), ())), preferred_element_type=F32)


def dot_nt(a, b):
    return lax.dot_general(a, b, (((1,), (1,)), ((), ())), preferred_element_type=F32)


def dot_tn(a, b):
    return lax.dot_general(a, b, (((0,), (0,)), ((), ())), preferred_element_type=F32)


def low_lanes(shape):
    return lax.broadcasted_iota(jnp.int32, shape, 1) < C


def conv_pair(weight_ref):
    weight = weight_ref[...].astype(F32)
    turned = pltpu.roll(weight, C, 1)
    low = low_lanes(weight.shape)
    even = jnp.concatenate([jnp.where(low, weight, 0.0), jnp.where(low, turned, 0.0)], axis=1)
    odd = jnp.concatenate([jnp.where(low, 0.0, turned), jnp.where(low, 0.0, weight)], axis=1)
    return jnp.concatenate([even[:C], odd[:C], even[C:], odd[C:]], axis=0).astype(BF16)


def mix_pair(weight_ref):
    weight = weight_ref[...].astype(F32)
    twice = jnp.concatenate([weight, weight], axis=1)
    low = low_lanes(twice.shape)
    even, odd = jnp.where(low, twice, 0.0), jnp.where(low, 0.0, twice)
    return jnp.concatenate([even[:C], odd[:C], even[C:], odd[C:]], axis=0).astype(BF16)


def live_values(values_ref, count_ref):
    groups = count_ref.shape[0]
    slots = values_ref.shape[1]
    cap = slots // groups
    me = lax.axis_index("node")
    column = lax.broadcasted_iota(jnp.int32, (8, slots), 1)
    limit = jnp.zeros((8, slots), jnp.int32)
    for p in range(groups):
        limit = jnp.where(column >= p * cap, p * cap + count_ref[p, me], limit)
    alive = (column < limit)[:1]
    return jnp.where(alive, values_ref[...].astype(F32), 0.0).astype(BF16)


def picker(rows_ref, nodes):
    slots = rows_ref.shape[1]
    node = lax.broadcasted_iota(jnp.int32, (nodes, slots), 0)
    return jnp.where(node == rows_ref[...], 1.0, 0.0).astype(BF16)


def gates(series_ref, delayed_ref, weight, bias_ref, j):
    bias = bias_ref[...]
    turned = pltpu.roll(jnp.broadcast_to(bias, (8, PAIR)), C, 1)[:1]
    low = low_lanes(bias.shape)
    both = jnp.concatenate([jnp.where(low, bias, turned), jnp.where(low, turned, bias)], axis=1)
    cols = pl.ds(j * PAIR, PAIR)
    stacked = jnp.concatenate([delayed_ref[:, cols], series_ref[:, cols]], axis=1)
    preact = dot(stacked, weight) + both
    return jnp.tanh(preact[:, :PAIR]), jax.nn.sigmoid(preact[:, PAIR:])


def slot_grads_kernel(cot_ref, mix_ref, values_ref, count_ref, out_ref):
    mix = mix_pair(mix_ref)
    live = live_values(values_ref, count_ref)
    for j in range(cot_ref.shape[1] // PAIR):
        cols = pl.ds(j * PAIR, PAIR)
        mixed_grad = dot_nt(cot_ref[:, cols], mix[PAIR:]).astype(BF16)
        out_ref[:, cols] = dot_tn(live, mixed_grad).astype(BF16)


def hidden_kernel(series_ref, delayed_ref, conv_ref, bias_ref, rows_ref, hidden_ref, out_ref):
    weight = conv_pair(conv_ref)
    pick = picker(rows_ref, series_ref.shape[0])
    for j in range(series_ref.shape[1] // PAIR):
        cols = pl.ds(j * PAIR, PAIR)
        filtered, opened = gates(series_ref, delayed_ref, weight, bias_ref, j)
        hidden = (filtered * opened).astype(BF16)
        hidden_ref[:, cols] = hidden
        out_ref[:, cols] = dot_tn(pick, hidden).astype(BF16)


def local_grad_kernel(cot_ref, mix_ref, local_ref, blocks_ref, out_ref):
    mix = mix_pair(mix_ref)
    tiles, per_tile, size, _ = local_ref.shape
    kept = []
    for j in range(cot_ref.shape[1] // PAIR):
        cols = pl.ds(j * PAIR, PAIR)
        grads = dot_nt(cot_ref[:, cols], mix)
        out_ref[:, cols] = grads[:, :PAIR]
        kept.append(grads[:, PAIR:].astype(BF16))
    mixed_grad = jnp.concatenate(kept, axis=1)
    for t in range(tiles):
        for b in range(per_tile):
            rows = pl.ds(pl.multiple_of(blocks_ref[t, b] * size, size), size)
            out_ref[rows, :] += dot_tn(local_ref[t, b], mixed_grad[t * size : (t + 1) * size])


def mixed_kernel(
    series_ref, hidden_ref, slots_ref, mix_ref, local_ref, blocks_ref, values_ref, count_ref, out_ref
):
    mix = mix_pair(mix_ref)
    live = live_values(values_ref, count_ref)
    tiles, per_tile, size, _ = local_ref.shape
    remote = dot(live, slots_ref[...])
    sums = []
    for t in range(tiles):
        total = remote[t * size : (t + 1) * size]
        for b in range(per_tile):
            rows = pl.ds(pl.multiple_of(blocks_ref[t, b] * size, size), size)
            total += dot(local_ref[t, b], hidden_ref[rows, :])
        sums.append(total.astype(BF16))
    mixed = jnp.concatenate(sums, axis=0)
    for j in range(series_ref.shape[1] // PAIR):
        cols = pl.ds(j * PAIR, PAIR)
        both = jnp.concatenate([hidden_ref[:, cols], mixed[:, j * PAIR : (j + 1) * PAIR]], axis=1)
        out_ref[:, cols] = (series_ref[:, cols].astype(F32) + dot(both, mix)).astype(BF16)


def conv_grad_kernel(
    series_ref, delayed_ref, conv_ref, bias_ref, rows_ref, partial_ref, back_ref, before_ref, now_ref
):
    weight = conv_pair(conv_ref)
    pick = picker(rows_ref, series_ref.shape[0])
    for j in range(series_ref.shape[1] // PAIR):
        cols = pl.ds(j * PAIR, PAIR)
        upstream = partial_ref[:, cols] + dot(pick, back_ref[:, cols])
        upstream = upstream.astype(BF16).astype(F32)
        filtered, opened = gates(series_ref, delayed_ref, weight, bias_ref, j)
        first = upstream * opened * (1.0 - filtered * filtered)
        second = upstream * filtered * opened * (1.0 - opened)
        gate_grad = jnp.concatenate([first, second], axis=1).astype(BF16)
        back = dot_nt(gate_grad, weight)
        before_ref[:, cols] = back[:, :PAIR].astype(BF16)
        now_ref[:, cols] = back[:, PAIR:]


def input_grad_kernel(cot_ref, now_ref, later_ref, out_ref):
    grad = (now_ref[...] + later_ref[...].astype(F32)).astype(BF16)
    out_ref[...] = (cot_ref[...].astype(F32) + grad.astype(F32)).astype(BF16)


VMEM = pl.BlockSpec(memory_space=pltpu.VMEM)
SMEM = pl.BlockSpec(memory_space=pltpu.SMEM)


def call(kernel, specs, outs, flops, *args):
    many = isinstance(outs, tuple)
    return pl.pallas_call(
        kernel,
        out_shape=outs,
        in_specs=specs,
        out_specs=tuple(VMEM for _ in outs) if many else VMEM,
        compiler_params=pltpu.CompilerParams(vmem_limit_bytes=32 << 20),
        cost_estimate=pl.CostEstimate(flops=flops, bytes_accessed=1 << 20, transcendentals=0),
    )(*args)


def local(
    series,
    conv_weight,
    conv_bias,
    mix_weight,
    local_blocks,
    local_values,
    send_rows,
    send_count,
    remote_values,
    cotangent,
):
    nodes, columns = series.shape
    groups = send_rows.shape[1]
    cap = send_rows.shape[2]
    half = 16
    rows_bf = jax.ShapeDtypeStruct((nodes, columns), BF16)
    rows_f32 = jax.ShapeDtypeStruct((nodes, columns), F32)
    own_rows = send_rows.reshape(1, -1)
    bias = conv_bias.reshape(1, -1)

    def exchange(x):
        y = lax.all_to_all(x.reshape(groups, cap, columns), "node", 0, 0, tiled=True)
        return y.reshape(groups * cap, columns)

    delayed = lax.ppermute(series, "tm", [(i, i + half) for i in range(half)])
    slot_grads = call(
        slot_grads_kernel, [VMEM, VMEM, VMEM, SMEM], rows_bf, 100 << 20, cotangent, mix_weight, remote_values, send_count
    )
    back_rows = exchange(slot_grads)
    partial = call(
        local_grad_kernel, [VMEM, VMEM, VMEM, SMEM], rows_f32, 100 << 20, cotangent, mix_weight, local_values, local_blocks
    )
    hidden, outgoing = call(
        hidden_kernel,
        [VMEM] * 5,
        (rows_bf, rows_bf),
        100 << 20,
        series,
        delayed,
        conv_weight,
        bias,
        own_rows,
    )
    slots = exchange(outgoing)
    before, now = call(
        conv_grad_kernel,
        [VMEM] * 7,
        (rows_bf, rows_f32),
        100 << 20,
        series,
        delayed,
        conv_weight,
        bias,
        own_rows,
        partial,
        back_rows,
    )
    later = lax.ppermute(before, "tm", [(i + half, i) for i in range(half)])
    mixed_out = call(
        mixed_kernel,
        [VMEM] * 5 + [SMEM, VMEM, SMEM],
        rows_bf,
        100 << 20,
        series,
        hidden,
        slots,
        mix_weight,
        local_values,
        local_blocks,
        remote_values,
        send_count,
    )
    input_grad = call(input_grad_kernel, [VMEM] * 3, rows_bf, 1 << 20, cotangent, now, later)
    return (mixed_out, input_grad)


def solution(mesh):
    in_specs = (
        P("node", "tm"),
        P(),
        P(),
        P(),
        P("node", None),
        P("node", None, None, None),
        P("node", None, None),
        P(),
        P("node", None),
        P("node", "tm"),
    )
    out_specs = (P("node", "tm"), P("node", "tm"))
    return jax.shard_map(local, mesh=mesh, in_specs=in_specs, out_specs=out_specs, check_vma=False)
```

```python
import jax
import jax.numpy as jnp
from jax import lax
from jax.experimental import pallas as pl
from jax.experimental.pallas import tpu as pltpu
from jax.sharding import PartitionSpec as P

C = 64
PAIR = 2 * C
F32 = jnp.float32
BF16 = jnp.bfloat16


def dot(a, b):
    return lax.dot_general(a, b, (((1,), (0,)), ((), ())), preferred_element_type=F32)


def dot_nt(a, b):
    return lax.dot_general(a, b, (((1,), (1,)), ((), ())), preferred_element_type=F32)


def dot_tn(a, b):
    return lax.dot_general(a, b, (((0,), (0,)), ((), ())), preferred_element_type=F32)


def iota(shape, dim):
    return lax.broadcasted_iota(jnp.int32, shape, dim)


def two_steps(weight):
    weight = weight.astype(F32)
    turned = pltpu.roll(weight, C, 1)
    low = iota(weight.shape, 1) < C
    even = jnp.concatenate([jnp.where(low, weight, 0.0), jnp.where(low, turned, 0.0)], axis=1)
    odd = jnp.concatenate([jnp.where(low, 0.0, turned), jnp.where(low, 0.0, weight)], axis=1)
    return jnp.concatenate([even, odd], axis=0).astype(BF16)


def conv_pair(conv_ref):
    return jnp.concatenate([two_steps(conv_ref[:C]), two_steps(conv_ref[C:])], axis=0)


def bias_pair(bias_ref):
    bias = bias_ref[...]
    turned = pltpu.roll(jnp.broadcast_to(bias, (8, PAIR)), C, 1)[:1]
    low = iota(bias.shape, 1) < C
    return jnp.concatenate([jnp.where(low, bias, turned), jnp.where(low, turned, bias)], axis=1)


def spread(table, slots):
    groups, cap = table.shape
    spot = iota((cap, slots), 1)
    place = jnp.where(lax.rem(spot, cap) == iota((cap, slots), 0), 1.0, 0.0).astype(BF16)
    wide = dot(table.astype(F32).astype(BF16), place)
    mine = iota((groups, slots), 1) // cap == iota((groups, slots), 0)
    return jnp.sum(jnp.where(mine, wide, 0.0), axis=0, keepdims=True)


def picker(rows_ref, nodes, slots):
    rows = spread(rows_ref[0], slots)
    return jnp.where(iota((nodes, slots), 0).astype(F32) == rows, 1.0, 0.0).astype(BF16)


def live_values(values_ref, count_ref):
    groups = count_ref.shape[0]
    slots = values_ref.shape[1]
    cap = slots // groups
    me = lax.axis_index("node")
    counts = count_ref[...].astype(F32)
    counts = jnp.where(iota(counts.shape, 1) == me, counts, 0.0)
    counts = jnp.sum(counts, axis=1, keepdims=True)
    column = iota((groups, slots), 1)
    mine = column // cap == iota((groups, slots), 0)
    limit = jnp.sum(jnp.where(mine, counts, 0.0), axis=0, keepdims=True)
    alive = lax.rem(column, cap)[:1].astype(F32) < limit
    return jnp.where(alive, values_ref[...].astype(F32), 0.0).astype(BF16)


def tanh_sigmoid(preact):
    filtered = jnp.tanh(preact[:, :PAIR])
    opened = 0.5 * jnp.tanh(0.5 * preact[:, PAIR:]) + 0.5
    return filtered, opened


def pairs(columns):
    return [slice(at, at + PAIR) for at in range(0, columns, PAIR)]


def wides(columns):
    return [slice(2 * at, 2 * at + 2 * PAIR) for at in range(0, columns, PAIR)]


def send_kernel(
    rows_hbm,
    series_hbm,
    mix_hbm,
    cot_hbm,
    count_hbm,
    values_hbm,
    out_hbm,
    rows_ref,
    series_ref,
    mix_ref,
    cot_ref,
    count_ref,
    values_ref,
    out_ref,
    came,
    gone,
):
    nodes, columns = series_ref.shape
    _, groups, cap, _ = out_ref.shape
    slots = groups * cap
    brought = [
        pltpu.make_async_copy(source, target, came.at[n])
        for n, (source, target) in enumerate(
            [
                (rows_hbm, rows_ref),
                (series_hbm, series_ref),
                (mix_hbm, mix_ref),
                (cot_hbm, cot_ref),
                (count_hbm, count_ref),
                (values_hbm, values_ref),
            ]
        )
    ]
    for copy in brought:
        copy.start()
    sent = [
        pltpu.make_async_copy(out_ref.at[n], out_hbm.at[:, pl.ds(n * cap, cap), :], gone.at[n])
        for n in range(2)
    ]
    brought[0].wait()
    pick = picker(rows_ref, nodes, slots)
    brought[1].wait()
    listed = dot_tn(pick, series_ref[...]).astype(BF16)
    out_ref[0] = listed.reshape(groups, cap, columns)
    sent[0].start()
    brought[2].wait()
    mix = two_steps(mix_ref[...])[:, PAIR:]
    brought[3].wait()
    mixed_grad = jnp.concatenate([dot(cot_ref[:, c], mix).astype(BF16) for c in pairs(columns)], axis=1)
    brought[4].wait()
    brought[5].wait()
    live = live_values(values_ref, count_ref)
    returned = dot_tn(live, mixed_grad).astype(BF16)
    out_ref[1] = returned.reshape(groups, cap, columns)
    sent[1].start()
    sent[0].wait()
    sent[1].wait()


def local_grad_kernel(
    cot_ref,
    mix_ref,
    local_ref,
    rows_ref,
    values_ref,
    count_ref,
    blocks_ref,
    out_ref,
    pick_ref,
    live_ref,
):
    nodes, slots = values_ref.shape
    pick_ref[...] = picker(rows_ref, nodes, slots)
    live_ref[...] = live_values(values_ref, count_ref)
    mix = two_steps(mix_ref[...])
    tiles, per_tile, size, _ = local_ref.shape
    kept = []
    for c in pairs(cot_ref.shape[1]):
        grads = dot(cot_ref[:, c], mix)
        out_ref[:, c] = grads[:, :PAIR]
        kept.append(grads[:, PAIR:].astype(BF16))
    mixed_grad = jnp.concatenate(kept, axis=1)
    for t in range(tiles):
        for b in range(per_tile):
            rows = pl.ds(pl.multiple_of(blocks_ref[t, b] * size, size), size)
            out_ref[rows, :] += dot_tn(local_ref[t, b], mixed_grad[t * size : (t + 1) * size])


def own_kernel(
    series_ref,
    delayed_ref,
    conv_ref,
    bias_ref,
    mix_ref,
    local_ref,
    blocks_ref,
    base_ref,
    slope_ref,
    weight_ref,
    bias_out_ref,
    mix_out_ref,
    hidden_ref,
):
    weight = conv_pair(conv_ref)
    bias = bias_pair(bias_ref)
    mix = two_steps(mix_ref[...])
    weight_ref[...] = weight
    bias_out_ref[...] = jnp.broadcast_to(bias, bias_out_ref.shape)
    mix_out_ref[...] = mix[:, PAIR:]
    tiles, per_tile, size, _ = local_ref.shape
    columns = series_ref.shape[1]
    for c, w in zip(pairs(columns), wides(columns)):
        stacked = jnp.concatenate([delayed_ref[:, c], series_ref[:, c]], axis=1)
        filtered, opened = tanh_sigmoid(dot(stacked, weight) + bias)
        hidden_ref[:, c] = (filtered * opened).astype(BF16)
        first = opened * (1.0 - filtered * filtered)
        second = filtered * opened * (1.0 - opened)
        slope_ref[:, w] = jnp.concatenate([first, second], axis=1)
    sums = []
    for t in range(tiles):
        total = None
        for b in range(per_tile):
            rows = pl.ds(pl.multiple_of(blocks_ref[t, b] * size, size), size)
            term = dot(local_ref[t, b], hidden_ref[rows, :])
            total = term if total is None else total + term
        sums.append(total.astype(BF16))
    local_sum = jnp.concatenate(sums, axis=0)
    for c in pairs(columns):
        both = jnp.concatenate([hidden_ref[:, c], local_sum[:, c]], axis=1)
        base_ref[:, c] = series_ref[:, c].astype(F32) + dot_nt(both, mix)


def gate_grad_kernel(got_ref, partial_ref, slope_ref, pick_ref, weight_ref, gate_ref, swap_ref):
    groups, both, columns = got_ref.shape
    cap = both // 2
    second_half = lax.axis_index("tm") >= lax.axis_size("tm") // 2
    back = got_ref[:, cap:, :].reshape(groups * cap, columns)
    upstream = (partial_ref[...] + dot(pick_ref[...], back)).astype(BF16).astype(F32)
    for c, w in zip(pairs(columns), wides(columns)):
        up = upstream[:, c]
        gate_ref[:, w] = (jnp.concatenate([up, up], axis=1) * slope_ref[:, w]).astype(BF16)

    @pl.when(second_half)
    def _():
        for c, w in zip(pairs(columns), wides(columns)):
            swap_ref[:, c] = dot_nt(gate_ref[:, w], weight_ref[:PAIR]).astype(BF16)

    @pl.when(jnp.logical_not(second_half))
    def _():
        swap_ref[...] = got_ref[:, :cap, :].reshape(groups * cap, columns)


def now_kernel(gate_ref, weight_ref, now_ref):
    columns = now_ref.shape[1]
    for c, w in zip(pairs(columns), wides(columns)):
        now_ref[:, c] = dot_nt(gate_ref[:, w], weight_ref[PAIR:])


def last_kernel(
    came_ref,
    got_ref,
    now_ref,
    live_ref,
    base_ref,
    cot_ref,
    weight_ref,
    bias_ref,
    mix_ref,
    out_ref,
    grad_ref,
):
    groups, both, columns = got_ref.shape
    cap = both // 2
    second_half = lax.axis_index("tm") >= lax.axis_size("tm") // 2
    came = came_ref[jnp.where(second_half, 0, 1)].astype(F32)
    later = jnp.where(second_half, 0.0, came)
    grad = (now_ref[...] + later).astype(BF16)
    grad_ref[...] = (cot_ref[...].astype(F32) + grad.astype(F32)).astype(BF16)
    before = jnp.where(second_half, came, 0.0).astype(BF16)
    listed = got_ref[:, :cap, :].reshape(groups * cap, columns)
    for c in pairs(columns):
        stacked = jnp.concatenate([before[:, c], listed[:, c]], axis=1)
        filtered, opened = tanh_sigmoid(dot(stacked, weight_ref[...]) + bias_ref[:1])
        hidden = (filtered * opened).astype(BF16)
        mixed = dot(live_ref[...], hidden).astype(BF16)
        out_ref[:, c] = (base_ref[:, c] + dot_nt(mixed, mix_ref[...])).astype(BF16)


VMEM = pl.BlockSpec(memory_space=pltpu.VMEM)
SMEM = pl.BlockSpec(memory_space=pltpu.SMEM)
HBM = pl.BlockSpec(memory_space=pltpu.HBM)


def call(kernel, outs, *args, scalars=(), ins=VMEM, out=VMEM, scratch=(), limit=32):
    many = isinstance(outs, tuple)
    return pl.pallas_call(
        kernel,
        out_shape=outs,
        in_specs=[SMEM if n in scalars else ins for n in range(len(args))],
        out_specs=tuple(out for _ in outs) if many else out,
        scratch_shapes=scratch,
        compiler_params=pltpu.CompilerParams(vmem_limit_bytes=limit << 20),
        cost_estimate=pl.CostEstimate(flops=1 << 27, bytes_accessed=1 << 21, transcendentals=0),
    )(*args)


def local(
    series,
    conv_weight,
    conv_bias,
    mix_weight,
    local_blocks,
    local_values,
    send_rows,
    send_count,
    remote_values,
    cotangent,
):
    nodes, columns = series.shape
    groups, cap = send_rows.shape[1:]
    slots = groups * cap
    places = lax.axis_size("tm")
    half = places // 2

    def shape(rows, cols, kind):
        return jax.ShapeDtypeStruct((rows, cols), kind)

    mix = mix_weight.T
    bias = conv_bias.reshape(1, -1)
    first = (send_rows, series, mix, cotangent, send_count, remote_values)
    send = call(
        send_kernel,
        jax.ShapeDtypeStruct((groups, 2 * cap, columns), BF16),
        *first,
        ins=HBM,
        out=HBM,
        limit=60,
        scratch=[pltpu.VMEM(a.shape, a.dtype) for a in first]
        + [
            pltpu.VMEM((2, groups, cap, columns), BF16),
            pltpu.SemaphoreType.DMA((len(first),)),
            pltpu.SemaphoreType.DMA((2,)),
        ],
    )
    got = lax.all_to_all(send, "node", 0, 0, tiled=True)
    delayed = lax.ppermute(series, "tm", [(i, i + half) for i in range(half)])
    partial, pick, live = call(
        local_grad_kernel,
        (shape(nodes, columns, F32), shape(nodes, slots, BF16), shape(nodes, slots, BF16)),
        cotangent,
        mix,
        local_values,
        send_rows,
        remote_values,
        send_count,
        local_blocks,
        scalars=(6,),
    )
    base, slope, weight, bias_wide, mix_mixed = call(
        own_kernel,
        (
            shape(nodes, columns, F32),
            shape(nodes, 2 * columns, F32),
            shape(2 * PAIR, 2 * PAIR, BF16),
            shape(8, 2 * PAIR, F32),
            shape(PAIR, PAIR, BF16),
        ),
        series,
        delayed,
        conv_weight,
        bias,
        mix,
        local_values,
        local_blocks,
        scalars=(6,),
        scratch=[pltpu.VMEM((nodes, columns), BF16)],
    )
    gate, swap = call(
        gate_grad_kernel,
        (shape(nodes, 2 * columns, BF16), shape(nodes, columns, BF16)),
        got,
        partial,
        slope,
        pick,
        weight,
    )
    came = lax.all_gather(swap, "tm", axis_index_groups=[[i, i + half] for i in range(half)])
    now = call(now_kernel, shape(nodes, columns, F32), gate, weight)
    return call(
        last_kernel,
        (shape(nodes, columns, BF16), shape(nodes, columns, BF16)),
        came,
        got,
        now,
        live,
        base,
        cotangent,
        weight,
        bias_wide,
        mix_mixed,
    )


def solution(mesh):
    in_specs = (
        P("node", "tm"),
        P(),
        P(),
        P(),
        P("node", None),
        P("node", None, None, None),
        P("node", None, None),
        P(),
        P("node", None),
        P("node", "tm"),
    )
    out_specs = (P("node", "tm"), P("node", "tm"))
    return jax.shard_map(local, mesh=mesh, in_specs=in_specs, out_specs=out_specs, check_vma=False)
```

```python
import jax
import jax.numpy as jnp
from jax import lax
from jax.experimental import pallas as pl
from jax.experimental.pallas import tpu as pltpu
from jax.sharding import PartitionSpec as P

C = 64
PAIR = 2 * C
F32 = jnp.float32
BF16 = jnp.bfloat16
FIRST = 12


def dot(a, b):
    return lax.dot_general(a, b, (((1,), (0,)), ((), ())), preferred_element_type=F32)


def dot_nt(a, b):
    return lax.dot_general(a, b, (((1,), (1,)), ((), ())), preferred_element_type=F32)


def dot_tn(a, b):
    return lax.dot_general(a, b, (((0,), (0,)), ((), ())), preferred_element_type=F32)


def iota(shape, dim):
    return lax.broadcasted_iota(jnp.int32, shape, dim)


def two_steps(weight):
    weight = weight.astype(F32)
    turned = pltpu.roll(weight, C, 1)
    low = iota(weight.shape, 1) < C
    even = jnp.concatenate([jnp.where(low, weight, 0.0), jnp.where(low, turned, 0.0)], axis=1)
    odd = jnp.concatenate([jnp.where(low, 0.0, turned), jnp.where(low, 0.0, weight)], axis=1)
    return jnp.concatenate([even, odd], axis=0).astype(BF16)


def conv_pair(conv_ref):
    return jnp.concatenate([two_steps(conv_ref[:C]), two_steps(conv_ref[C:])], axis=0)


def bias_pair(bias_ref):
    bias = bias_ref[...]
    turned = pltpu.roll(jnp.broadcast_to(bias, (8, PAIR)), C, 1)[:1]
    low = iota(bias.shape, 1) < C
    return jnp.concatenate([jnp.where(low, bias, turned), jnp.where(low, turned, bias)], axis=1)


def spread(table, slots):
    groups, cap = table.shape
    spot = iota((cap, slots), 1)
    place = jnp.where(lax.rem(spot, cap) == iota((cap, slots), 0), 1.0, 0.0).astype(BF16)
    wide = dot(table.astype(F32).astype(BF16), place)
    mine = iota((groups, slots), 1) // cap == iota((groups, slots), 0)
    return jnp.sum(jnp.where(mine, wide, 0.0), axis=0, keepdims=True)


def picker(rows_ref, nodes, slots):
    rows = spread(rows_ref[0], slots)
    return jnp.where(iota((nodes, slots), 0).astype(F32) == rows, 1.0, 0.0).astype(BF16)


def live_values(values_ref, count_ref):
    groups = count_ref.shape[0]
    slots = values_ref.shape[1]
    cap = slots // groups
    me = lax.axis_index("node")
    counts = count_ref[...].astype(F32)
    counts = jnp.where(iota(counts.shape, 1) == me, counts, 0.0)
    counts = jnp.sum(counts, axis=1, keepdims=True)
    column = iota((groups, slots), 1)
    mine = column // cap == iota((groups, slots), 0)
    limit = jnp.sum(jnp.where(mine, counts, 0.0), axis=0, keepdims=True)
    alive = lax.rem(column, cap)[:1].astype(F32) < limit
    return jnp.where(alive, values_ref[...].astype(F32), 0.0).astype(BF16)


def turned(blocks, first):
    first = first % blocks.shape[0]
    return jnp.concatenate([blocks[first:], blocks[:first]], axis=0) if first else blocks


def tanh_sigmoid(preact):
    filtered = jnp.tanh(preact[:, :PAIR])
    opened = 0.5 * jnp.tanh(0.5 * preact[:, PAIR:]) + 0.5
    return filtered, opened


def pairs(columns):
    return [slice(at, at + PAIR) for at in range(0, columns, PAIR)]


def wides(columns):
    return [slice(2 * at, 2 * at + 2 * PAIR) for at in range(0, columns, PAIR)]


def send_kernel(
    rows_hbm,
    series_hbm,
    mix_hbm,
    cot_hbm,
    count_hbm,
    values_hbm,
    out_hbm,
    rows_ref,
    series_ref,
    mix_ref,
    cot_ref,
    count_ref,
    values_ref,
    out_ref,
    came,
    gone,
):
    nodes, columns = series_ref.shape
    _, groups, cap, _ = out_ref.shape
    slots = groups * cap
    brought = [
        pltpu.make_async_copy(source, target, came.at[n])
        for n, (source, target) in enumerate(
            [
                (rows_hbm, rows_ref),
                (series_hbm, series_ref),
                (mix_hbm, mix_ref),
                (cot_hbm, cot_ref),
                (count_hbm, count_ref),
                (values_hbm, values_ref),
            ]
        )
    ]
    for copy in brought:
        copy.start()
    sent = [
        pltpu.make_async_copy(out_ref.at[n], out_hbm.at[:, pl.ds(n * cap, cap), :], gone.at[n])
        for n in range(2)
    ]
    for copy in brought:
        copy.wait()
    pick = picker(rows_ref, nodes, slots)
    live = live_values(values_ref, count_ref)
    mix = two_steps(mix_ref[...])[:, PAIR:]
    mixed_grad = jnp.concatenate([dot(cot_ref[:, c], mix).astype(BF16) for c in pairs(columns)], axis=1)
    listed = dot_tn(pick, series_ref[...]).astype(BF16)
    out_ref[0] = turned(listed.reshape(groups, cap, columns), FIRST)
    sent[0].start()
    returned = dot_tn(live, mixed_grad).astype(BF16)
    out_ref[1] = turned(returned.reshape(groups, cap, columns), FIRST)
    sent[1].start()
    sent[0].wait()
    sent[1].wait()


def local_grad_kernel(
    cot_ref,
    mix_ref,
    local_ref,
    rows_ref,
    values_ref,
    count_ref,
    blocks_ref,
    out_ref,
    slots_ref,
):
    nodes, slots = values_ref.shape
    slots_ref[:, :slots] = picker(rows_ref, nodes, slots)
    slots_ref[:, slots:] = live_values(values_ref, count_ref)
    mix = two_steps(mix_ref[...])
    tiles, per_tile, size, _ = local_ref.shape
    kept = []
    for c in pairs(cot_ref.shape[1]):
        grads = dot(cot_ref[:, c], mix)
        out_ref[:, c] = grads[:, :PAIR]
        kept.append(grads[:, PAIR:].astype(BF16))
    mixed_grad = jnp.concatenate(kept, axis=1)
    for t in range(tiles):
        for b in range(per_tile):
            rows = pl.ds(pl.multiple_of(blocks_ref[t, b] * size, size), size)
            out_ref[rows, :] += dot_tn(local_ref[t, b], mixed_grad[t * size : (t + 1) * size])


def own_kernel(
    series_ref,
    delayed_ref,
    conv_ref,
    bias_ref,
    mix_ref,
    local_ref,
    blocks_ref,
    base_ref,
    slope_ref,
    weight_ref,
    hidden_ref,
):
    weight = conv_pair(conv_ref)
    bias = bias_pair(bias_ref)
    mix = two_steps(mix_ref[...])
    weight_ref[: 2 * PAIR] = weight
    weight_ref[2 * PAIR :] = mix
    tiles, per_tile, size, _ = local_ref.shape
    columns = series_ref.shape[1]
    for c, w in zip(pairs(columns), wides(columns)):
        stacked = jnp.concatenate([delayed_ref[:, c], series_ref[:, c]], axis=1)
        filtered, opened = tanh_sigmoid(dot(stacked, weight) + bias)
        hidden_ref[:, c] = (filtered * opened).astype(BF16)
        first = opened * (1.0 - filtered * filtered)
        second = filtered * opened * (1.0 - opened)
        slope_ref[:, w] = jnp.concatenate([first, second], axis=1)
    sums = []
    for t in range(tiles):
        total = None
        for b in range(per_tile):
            rows = pl.ds(pl.multiple_of(blocks_ref[t, b] * size, size), size)
            term = dot(local_ref[t, b], hidden_ref[rows, :])
            total = term if total is None else total + term
        sums.append(total.astype(BF16))
    local_sum = jnp.concatenate(sums, axis=0)
    for c in pairs(columns):
        both = jnp.concatenate([hidden_ref[:, c], local_sum[:, c]], axis=1)
        base_ref[:, c] = series_ref[:, c].astype(F32) + dot_nt(both, mix)


def gate_grad_kernel(got_ref, partial_ref, slope_ref, slots_ref, weight_ref, gate_ref, swap_ref):
    groups, both, columns = got_ref.shape
    cap = both // 2
    second_half = lax.axis_index("tm") >= lax.axis_size("tm") // 2
    back = turned(got_ref[:, cap:, :], -FIRST).reshape(groups * cap, columns)
    upstream = (partial_ref[...] + dot(slots_ref[:, : groups * cap], back)).astype(BF16).astype(F32)
    for c, w in zip(pairs(columns), wides(columns)):
        up = upstream[:, c]
        gate_ref[:, w] = (jnp.concatenate([up, up], axis=1) * slope_ref[:, w]).astype(BF16)

    @pl.when(second_half)
    def _():
        for c, w in zip(pairs(columns), wides(columns)):
            swap_ref[:, c] = dot_nt(gate_ref[:, w], weight_ref[:PAIR]).astype(BF16)

    @pl.when(jnp.logical_not(second_half))
    def _():
        swap_ref[...] = turned(got_ref[:, :cap, :], -FIRST).reshape(groups * cap, columns)


def last_kernel(
    came_ref,
    got_ref,
    gate_ref,
    slots_ref,
    base_ref,
    cot_ref,
    weight_ref,
    bias_ref,
    out_hbm,
    grad_hbm,
    out_ref,
    grad_ref,
    gone,
):
    groups, both, columns = got_ref.shape
    cap = both // 2
    slots = groups * cap
    nodes = cot_ref.shape[0]
    second_half = lax.axis_index("tm") >= lax.axis_size("tm") // 2
    came = came_ref[jnp.where(second_half, 0, 1)].astype(F32)
    later = jnp.where(second_half, 0.0, came)
    for c, w in zip(pairs(columns), wides(columns)):
        grad = (dot_nt(gate_ref[:, w], weight_ref[PAIR : 2 * PAIR]) + later[:, c]).astype(BF16)
        grad_ref[:, c] = (cot_ref[:, c].astype(F32) + grad.astype(F32)).astype(BF16)
    grad_copy = pltpu.make_async_copy(grad_ref, grad_hbm, gone.at[0])
    grad_copy.start()
    before = jnp.where(second_half, came, 0.0).astype(BF16)
    listed = turned(got_ref[:, :cap, :], -FIRST).reshape(slots, columns)
    bias = bias_pair(bias_ref)
    kept = []
    for c in pairs(columns):
        stacked = jnp.concatenate([before[:, c], listed[:, c]], axis=1)
        filtered, opened = tanh_sigmoid(dot(stacked, weight_ref[: 2 * PAIR]) + bias)
        kept.append((filtered * opened).astype(BF16))
    hidden = jnp.concatenate(kept, axis=1)
    copies = []
    for n in range(2):
        rows = pl.ds(n * (nodes // 2), nodes // 2)
        mixed = dot(slots_ref[rows, slots:], hidden).astype(BF16)
        for c in pairs(columns):
            added = dot_nt(mixed[:, c], weight_ref[2 * PAIR :, PAIR:])
            out_ref[rows, c] = (base_ref[rows, c] + added).astype(BF16)
        copies.append(pltpu.make_async_copy(out_ref.at[rows], out_hbm.at[rows], gone.at[n + 1]))
        copies[n].start()
    grad_copy.wait()
    for copy in copies:
        copy.wait()


VMEM = pl.BlockSpec(memory_space=pltpu.VMEM)
SMEM = pl.BlockSpec(memory_space=pltpu.SMEM)
HBM = pl.BlockSpec(memory_space=pltpu.HBM)


def call(kernel, outs, *args, scalars=(), ins=VMEM, out=VMEM, scratch=(), limit=32):
    many = isinstance(outs, tuple)
    return pl.pallas_call(
        kernel,
        out_shape=outs,
        in_specs=[SMEM if n in scalars else ins for n in range(len(args))],
        out_specs=tuple(out for _ in outs) if many else out,
        scratch_shapes=scratch,
        compiler_params=pltpu.CompilerParams(vmem_limit_bytes=limit << 20),
        cost_estimate=pl.CostEstimate(flops=1 << 27, bytes_accessed=1 << 21, transcendentals=0),
    )(*args)


def local(
    series,
    conv_weight,
    conv_bias,
    mix_weight,
    local_blocks,
    local_values,
    send_rows,
    send_count,
    remote_values,
    cotangent,
):
    nodes, columns = series.shape
    groups, cap = send_rows.shape[1:]
    slots = groups * cap
    places = lax.axis_size("tm")
    half = places // 2

    def shape(rows, cols, kind):
        return jax.ShapeDtypeStruct((rows, cols), kind)

    mix = mix_weight.T
    bias = conv_bias.reshape(1, -1)
    first = (send_rows, series, mix, cotangent, send_count, remote_values)
    send = call(
        send_kernel,
        jax.ShapeDtypeStruct((groups, 2 * cap, columns), BF16),
        *first,
        ins=HBM,
        out=HBM,
        limit=60,
        scratch=[pltpu.VMEM(a.shape, a.dtype) for a in first]
        + [
            pltpu.VMEM((2, groups, cap, columns), BF16),
            pltpu.SemaphoreType.DMA((len(first),)),
            pltpu.SemaphoreType.DMA((2,)),
        ],
    )
    order = [(FIRST + k) % groups for k in range(groups)]
    got = lax.all_to_all(send, "node", 0, 0, axis_index_groups=[order], tiled=True)
    delayed = lax.ppermute(series, "tm", [(i, i + half) for i in range(half)])
    partial, picked_live = call(
        local_grad_kernel,
        (shape(nodes, columns, F32), shape(nodes, 2 * slots, BF16)),
        cotangent,
        mix,
        local_values,
        send_rows,
        remote_values,
        send_count,
        local_blocks,
        scalars=(6,),
    )
    base, slope, weight = call(
        own_kernel,
        (shape(nodes, columns, F32), shape(nodes, 2 * columns, F32), shape(3 * PAIR, 2 * PAIR, BF16)),
        series,
        delayed,
        conv_weight,
        bias,
        mix,
        local_values,
        local_blocks,
        scalars=(6,),
        scratch=[pltpu.VMEM((nodes, columns), BF16)],
    )
    gate, swap = call(
        gate_grad_kernel,
        (shape(nodes, 2 * columns, BF16), shape(nodes, columns, BF16)),
        got,
        partial,
        slope,
        picked_live,
        weight,
    )
    came = lax.all_gather(swap, "tm", axis_index_groups=[[i, i + half] for i in range(half)])
    return call(
        last_kernel,
        (shape(nodes, columns, BF16), shape(nodes, columns, BF16)),
        came,
        got,
        gate,
        picked_live,
        base,
        cotangent,
        weight,
        bias,
        out=HBM,
        scratch=[
            pltpu.VMEM((nodes, columns), BF16),
            pltpu.VMEM((nodes, columns), BF16),
            pltpu.SemaphoreType.DMA((3,)),
        ],
    )


def solution(mesh):
    in_specs = (
        P("node", "tm"),
        P(),
        P(),
        P(),
        P("node", None),
        P("node", None, None, None),
        P("node", None, None),
        P(),
        P("node", None),
        P("node", "tm"),
    )
    out_specs = (P("node", "tm"), P("node", "tm"))
    return jax.shard_map(local, mesh=mesh, in_specs=in_specs, out_specs=out_specs, check_vma=False)
```

```python
import jax
import jax.numpy as jnp
from jax import lax
from jax.experimental import pallas as pl
from jax.experimental.pallas import tpu as pltpu
from jax.sharding import PartitionSpec as P

C = 64
PAIR = 2 * C
F32 = jnp.float32
BF16 = jnp.bfloat16
FIRST = 11
ORDER = tuple((FIRST + (k + 1) // 2 * (1 if k % 2 else -1)) % 16 for k in range(16))


def dot(a, b):
    return lax.dot_general(a, b, (((1,), (0,)), ((), ())), preferred_element_type=F32)


def dot_nt(a, b):
    return lax.dot_general(a, b, (((1,), (1,)), ((), ())), preferred_element_type=F32)


def dot_tn(a, b):
    return lax.dot_general(a, b, (((0,), (0,)), ((), ())), preferred_element_type=F32)


def iota(shape, dim):
    return lax.broadcasted_iota(jnp.int32, shape, dim)


def two_steps(weight):
    weight = weight.astype(F32)
    turned = pltpu.roll(weight, C, 1)
    low = iota(weight.shape, 1) < C
    even = jnp.concatenate([jnp.where(low, weight, 0.0), jnp.where(low, turned, 0.0)], axis=1)
    odd = jnp.concatenate([jnp.where(low, 0.0, turned), jnp.where(low, 0.0, weight)], axis=1)
    return jnp.concatenate([even, odd], axis=0).astype(BF16)


def conv_pair(conv_ref):
    return jnp.concatenate([two_steps(conv_ref[:C]), two_steps(conv_ref[C:])], axis=0)


def bias_pair(bias_ref):
    bias = bias_ref[...]
    turned = pltpu.roll(jnp.broadcast_to(bias, (8, PAIR)), C, 1)[:1]
    low = iota(bias.shape, 1) < C
    return jnp.concatenate([jnp.where(low, bias, turned), jnp.where(low, turned, bias)], axis=1)


def spread(table, slots):
    groups, cap = table.shape
    spot = iota((cap, slots), 1)
    place = jnp.where(lax.rem(spot, cap) == iota((cap, slots), 0), 1.0, 0.0).astype(BF16)
    wide = dot(table.astype(F32).astype(BF16), place)
    mine = iota((groups, slots), 1) // cap == iota((groups, slots), 0)
    return jnp.sum(jnp.where(mine, wide, 0.0), axis=0, keepdims=True)


def picker(rows_ref, nodes, slots):
    rows = spread(rows_ref[0], slots)
    return jnp.where(iota((nodes, slots), 0).astype(F32) == rows, 1.0, 0.0).astype(BF16)


def live_values(values_ref, count_ref):
    groups = count_ref.shape[0]
    slots = values_ref.shape[1]
    cap = slots // groups
    me = lax.axis_index("node")
    counts = count_ref[...].astype(F32)
    counts = jnp.where(iota(counts.shape, 1) == me, counts, 0.0)
    counts = jnp.sum(counts, axis=1, keepdims=True)
    column = iota((groups, slots), 1)
    mine = column // cap == iota((groups, slots), 0)
    limit = jnp.sum(jnp.where(mine, counts, 0.0), axis=0, keepdims=True)
    alive = lax.rem(column, cap)[:1].astype(F32) < limit
    return jnp.where(alive, values_ref[...].astype(F32), 0.0).astype(BF16)


def to_order(blocks):
    return jnp.concatenate([blocks[q : q + 1] for q in ORDER], axis=0)


def from_order(blocks):
    places = [ORDER.index(q) for q in range(len(ORDER))]
    return jnp.concatenate([blocks[k : k + 1] for k in places], axis=0)


def tanh_sigmoid(preact):
    filtered = jnp.tanh(preact[:, :PAIR])
    opened = 0.5 * jnp.tanh(0.5 * preact[:, PAIR:]) + 0.5
    return filtered, opened


def pairs(columns):
    return [slice(at, at + PAIR) for at in range(0, columns, PAIR)]


def wides(columns):
    return [slice(2 * at, 2 * at + 2 * PAIR) for at in range(0, columns, PAIR)]


def send_kernel(
    rows_hbm,
    series_hbm,
    mix_hbm,
    cot_hbm,
    count_hbm,
    values_hbm,
    out_hbm,
    rows_ref,
    series_ref,
    mix_ref,
    cot_ref,
    count_ref,
    values_ref,
    out_ref,
    came,
    gone,
):
    nodes, columns = series_ref.shape
    _, groups, cap, _ = out_ref.shape
    slots = groups * cap
    brought = [
        pltpu.make_async_copy(source, target, came.at[n])
        for n, (source, target) in enumerate(
            [
                (rows_hbm, rows_ref),
                (series_hbm, series_ref),
                (mix_hbm, mix_ref),
                (cot_hbm, cot_ref),
                (count_hbm, count_ref),
                (values_hbm, values_ref),
            ]
        )
    ]
    for copy in brought:
        copy.start()
    sent = [
        pltpu.make_async_copy(out_ref.at[n], out_hbm.at[:, pl.ds(n * cap, cap), :], gone.at[n])
        for n in range(2)
    ]
    for copy in brought:
        copy.wait()
    pick = picker(rows_ref, nodes, slots)
    live = live_values(values_ref, count_ref)
    mix = two_steps(mix_ref[...])[:, PAIR:]
    mixed_grad = jnp.concatenate([dot(cot_ref[:, c], mix).astype(BF16) for c in pairs(columns)], axis=1)
    listed = dot_tn(pick, series_ref[...]).astype(BF16)
    out_ref[0] = to_order(listed.reshape(groups, cap, columns))
    sent[0].start()
    returned = dot_tn(live, mixed_grad).astype(BF16)
    out_ref[1] = to_order(returned.reshape(groups, cap, columns))
    sent[1].start()
    sent[0].wait()
    sent[1].wait()


def local_grad_kernel(
    cot_ref,
    mix_ref,
    local_ref,
    rows_ref,
    values_ref,
    count_ref,
    blocks_ref,
    out_ref,
    slots_ref,
):
    nodes, slots = values_ref.shape
    slots_ref[:, :slots] = picker(rows_ref, nodes, slots)
    slots_ref[:, slots:] = live_values(values_ref, count_ref)
    mix = two_steps(mix_ref[...])
    tiles, per_tile, size, _ = local_ref.shape
    kept = []
    for c in pairs(cot_ref.shape[1]):
        grads = dot(cot_ref[:, c], mix)
        out_ref[:, c] = grads[:, :PAIR]
        kept.append(grads[:, PAIR:].astype(BF16))
    mixed_grad = jnp.concatenate(kept, axis=1)
    for t in range(tiles):
        for b in range(per_tile):
            rows = pl.ds(pl.multiple_of(blocks_ref[t, b] * size, size), size)
            out_ref[rows, :] += dot_tn(local_ref[t, b], mixed_grad[t * size : (t + 1) * size])


def own_kernel(
    series_ref,
    delayed_ref,
    conv_ref,
    bias_ref,
    mix_ref,
    local_ref,
    blocks_ref,
    base_ref,
    slope_ref,
    weight_ref,
    hidden_ref,
):
    weight = conv_pair(conv_ref)
    bias = bias_pair(bias_ref)
    mix = two_steps(mix_ref[...])
    weight_ref[: 2 * PAIR] = weight
    weight_ref[2 * PAIR :] = mix
    tiles, per_tile, size, _ = local_ref.shape
    columns = series_ref.shape[1]
    for c, w in zip(pairs(columns), wides(columns)):
        stacked = jnp.concatenate([delayed_ref[:, c], series_ref[:, c]], axis=1)
        filtered, opened = tanh_sigmoid(dot(stacked, weight) + bias)
        hidden_ref[:, c] = (filtered * opened).astype(BF16)
        first = opened * (1.0 - filtered * filtered)
        second = filtered * opened * (1.0 - opened)
        slope_ref[:, w] = jnp.concatenate([first, second], axis=1)
    sums = []
    for t in range(tiles):
        total = None
        for b in range(per_tile):
            rows = pl.ds(pl.multiple_of(blocks_ref[t, b] * size, size), size)
            term = dot(local_ref[t, b], hidden_ref[rows, :])
            total = term if total is None else total + term
        sums.append(total.astype(BF16))
    local_sum = jnp.concatenate(sums, axis=0)
    for c in pairs(columns):
        both = jnp.concatenate([hidden_ref[:, c], local_sum[:, c]], axis=1)
        base_ref[:, c] = series_ref[:, c].astype(F32) + dot_nt(both, mix)


def gate_grad_kernel(got_ref, partial_ref, slope_ref, slots_ref, weight_ref, gate_ref, swap_ref):
    groups, both, columns = got_ref.shape
    cap = both // 2
    second_half = lax.axis_index("tm") >= lax.axis_size("tm") // 2
    back = from_order(got_ref[:, cap:, :]).reshape(groups * cap, columns)
    upstream = (partial_ref[...] + dot(slots_ref[:, : groups * cap], back)).astype(BF16).astype(F32)
    for c, w in zip(pairs(columns), wides(columns)):
        up = upstream[:, c]
        gate_ref[:, w] = (jnp.concatenate([up, up], axis=1) * slope_ref[:, w]).astype(BF16)

    @pl.when(second_half)
    def _():
        for c, w in zip(pairs(columns), wides(columns)):
            swap_ref[:, c] = dot_nt(gate_ref[:, w], weight_ref[:PAIR]).astype(BF16)

    @pl.when(jnp.logical_not(second_half))
    def _():
        swap_ref[...] = from_order(got_ref[:, :cap, :]).reshape(groups * cap, columns)


def last_kernel(
    came_ref,
    got_ref,
    gate_ref,
    slots_ref,
    base_ref,
    cot_ref,
    weight_ref,
    bias_ref,
    out_hbm,
    grad_hbm,
    out_ref,
    grad_ref,
    gone,
):
    groups, both, columns = got_ref.shape
    cap = both // 2
    slots = groups * cap
    nodes = cot_ref.shape[0]
    second_half = lax.axis_index("tm") >= lax.axis_size("tm") // 2
    came = came_ref[jnp.where(second_half, 0, 1)].astype(F32)
    later = jnp.where(second_half, 0.0, came)
    for c, w in zip(pairs(columns), wides(columns)):
        grad = (dot_nt(gate_ref[:, w], weight_ref[PAIR : 2 * PAIR]) + later[:, c]).astype(BF16)
        grad_ref[:, c] = (cot_ref[:, c].astype(F32) + grad.astype(F32)).astype(BF16)
    grad_copy = pltpu.make_async_copy(grad_ref, grad_hbm, gone.at[0])
    grad_copy.start()
    before = jnp.where(second_half, came, 0.0).astype(BF16)
    listed = from_order(got_ref[:, :cap, :]).reshape(slots, columns)
    bias = bias_pair(bias_ref)
    kept = []
    for c in pairs(columns):
        stacked = jnp.concatenate([before[:, c], listed[:, c]], axis=1)
        filtered, opened = tanh_sigmoid(dot(stacked, weight_ref[: 2 * PAIR]) + bias)
        kept.append((filtered * opened).astype(BF16))
    hidden = jnp.concatenate(kept, axis=1)
    copies = []
    for n in range(2):
        rows = pl.ds(n * (nodes // 2), nodes // 2)
        mixed = dot(slots_ref[rows, slots:], hidden).astype(BF16)
        for c in pairs(columns):
            added = dot_nt(mixed[:, c], weight_ref[2 * PAIR :, PAIR:])
            out_ref[rows, c] = (base_ref[rows, c] + added).astype(BF16)
        copies.append(pltpu.make_async_copy(out_ref.at[rows], out_hbm.at[rows], gone.at[n + 1]))
        copies[n].start()
    grad_copy.wait()
    for copy in copies:
        copy.wait()


VMEM = pl.BlockSpec(memory_space=pltpu.VMEM)
SMEM = pl.BlockSpec(memory_space=pltpu.SMEM)
HBM = pl.BlockSpec(memory_space=pltpu.HBM)


def call(kernel, outs, *args, scalars=(), ins=VMEM, out=VMEM, scratch=(), limit=32):
    many = isinstance(outs, tuple)
    return pl.pallas_call(
        kernel,
        out_shape=outs,
        in_specs=[SMEM if n in scalars else ins for n in range(len(args))],
        out_specs=tuple(out for _ in outs) if many else out,
        scratch_shapes=scratch,
        compiler_params=pltpu.CompilerParams(vmem_limit_bytes=limit << 20),
        cost_estimate=pl.CostEstimate(flops=1 << 27, bytes_accessed=1 << 21, transcendentals=0),
    )(*args)


def local(
    series,
    conv_weight,
    conv_bias,
    mix_weight,
    local_blocks,
    local_values,
    send_rows,
    send_count,
    remote_values,
    cotangent,
):
    nodes, columns = series.shape
    groups, cap = send_rows.shape[1:]
    slots = groups * cap
    places = lax.axis_size("tm")
    half = places // 2

    def shape(rows, cols, kind):
        return jax.ShapeDtypeStruct((rows, cols), kind)

    mix = mix_weight.T
    bias = conv_bias.reshape(1, -1)
    first = (send_rows, series, mix, cotangent, send_count, remote_values)
    send = call(
        send_kernel,
        jax.ShapeDtypeStruct((groups, 2 * cap, columns), BF16),
        *first,
        ins=HBM,
        out=HBM,
        limit=60,
        scratch=[pltpu.VMEM(a.shape, a.dtype) for a in first]
        + [
            pltpu.VMEM((2, groups, cap, columns), BF16),
            pltpu.SemaphoreType.DMA((len(first),)),
            pltpu.SemaphoreType.DMA((2,)),
        ],
    )
    got = lax.all_to_all(send, "node", 0, 0, axis_index_groups=[list(ORDER)], tiled=True)
    delayed = lax.ppermute(series, "tm", [(i, i + half) for i in range(half)])
    partial, picked_live = call(
        local_grad_kernel,
        (shape(nodes, columns, F32), shape(nodes, 2 * slots, BF16)),
        cotangent,
        mix,
        local_values,
        send_rows,
        remote_values,
        send_count,
        local_blocks,
        scalars=(6,),
    )
    base, slope, weight = call(
        own_kernel,
        (shape(nodes, columns, F32), shape(nodes, 2 * columns, F32), shape(3 * PAIR, 2 * PAIR, BF16)),
        series,
        delayed,
        conv_weight,
        bias,
        mix,
        local_values,
        local_blocks,
        scalars=(6,),
        scratch=[pltpu.VMEM((nodes, columns), BF16)],
    )
    gate, swap = call(
        gate_grad_kernel,
        (shape(nodes, 2 * columns, BF16), shape(nodes, columns, BF16)),
        got,
        partial,
        slope,
        picked_live,
        weight,
    )
    came = lax.all_gather(swap, "tm", axis_index_groups=[[i, i + half] for i in range(half)])
    return call(
        last_kernel,
        (shape(nodes, columns, BF16), shape(nodes, columns, BF16)),
        came,
        got,
        gate,
        picked_live,
        base,
        cotangent,
        weight,
        bias,
        out=HBM,
        scratch=[
            pltpu.VMEM((nodes, columns), BF16),
            pltpu.VMEM((nodes, columns), BF16),
            pltpu.SemaphoreType.DMA((3,)),
        ],
    )


def solution(mesh):
    in_specs = (
        P("node", "tm"),
        P(),
        P(),
        P(),
        P("node", None),
        P("node", None, None, None),
        P("node", None, None),
        P(),
        P("node", None),
        P("node", "tm"),
    )
    out_specs = (P("node", "tm"), P("node", "tm"))
    return jax.shard_map(local, mesh=mesh, in_specs=in_specs, out_specs=out_specs, check_vma=False)
```

```python
import jax
import jax.numpy as jnp
from jax import lax
from jax.experimental import pallas as pl
from jax.experimental.pallas import tpu as pltpu
from jax.sharding import PartitionSpec as P

C = 64
PAIR = 2 * C
F32 = jnp.float32
BF16 = jnp.bfloat16
ORDER = (11, 12, 6, 13, 9, 14, 8, 15, 7, 0, 10, 1, 5, 2, 4, 3)


def dot(a, b):
    return lax.dot_general(a, b, (((1,), (0,)), ((), ())), preferred_element_type=F32)


def dot_nt(a, b):
    return lax.dot_general(a, b, (((1,), (1,)), ((), ())), preferred_element_type=F32)


def dot_tn(a, b):
    return lax.dot_general(a, b, (((0,), (0,)), ((), ())), preferred_element_type=F32)


def iota(shape, dim):
    return lax.broadcasted_iota(jnp.int32, shape, dim)


def two_steps(weight):
    weight = weight.astype(F32)
    turned = pltpu.roll(weight, C, 1)
    low = iota(weight.shape, 1) < C
    even = jnp.concatenate([jnp.where(low, weight, 0.0), jnp.where(low, turned, 0.0)], axis=1)
    odd = jnp.concatenate([jnp.where(low, 0.0, turned), jnp.where(low, 0.0, weight)], axis=1)
    return jnp.concatenate([even, odd], axis=0).astype(BF16)


def conv_pair(conv_ref):
    return jnp.concatenate([two_steps(conv_ref[:C]), two_steps(conv_ref[C:])], axis=0)


def bias_pair(bias_ref):
    bias = bias_ref[...]
    turned = pltpu.roll(jnp.broadcast_to(bias, (8, PAIR)), C, 1)[:1]
    low = iota(bias.shape, 1) < C
    return jnp.concatenate([jnp.where(low, bias, turned), jnp.where(low, turned, bias)], axis=1)


def spread(table, slots):
    groups, cap = table.shape
    spot = iota((cap, slots), 1)
    place = jnp.where(lax.rem(spot, cap) == iota((cap, slots), 0), 1.0, 0.0).astype(BF16)
    wide = dot(table.astype(F32).astype(BF16), place)
    mine = iota((groups, slots), 1) // cap == iota((groups, slots), 0)
    return jnp.sum(jnp.where(mine, wide, 0.0), axis=0, keepdims=True)


def picker(rows_ref, nodes, slots):
    rows = spread(rows_ref[0], slots)
    return jnp.where(iota((nodes, slots), 0).astype(F32) == rows, 1.0, 0.0).astype(BF16)


def live_values(values_ref, count_ref):
    groups = count_ref.shape[0]
    slots = values_ref.shape[1]
    cap = slots // groups
    me = lax.axis_index("node")
    counts = count_ref[...].astype(F32)
    counts = jnp.where(iota(counts.shape, 1) == me, counts, 0.0)
    counts = jnp.sum(counts, axis=1, keepdims=True)
    column = iota((groups, slots), 1)
    mine = column // cap == iota((groups, slots), 0)
    limit = jnp.sum(jnp.where(mine, counts, 0.0), axis=0, keepdims=True)
    alive = lax.rem(column, cap)[:1].astype(F32) < limit
    return jnp.where(alive, values_ref[...].astype(F32), 0.0).astype(BF16)


def to_order(blocks):
    return jnp.concatenate([blocks[q : q + 1] for q in ORDER], axis=0)


def from_order(blocks):
    places = [ORDER.index(q) for q in range(len(ORDER))]
    return jnp.concatenate([blocks[k : k + 1] for k in places], axis=0)


def tanh_sigmoid(preact):
    filtered = jnp.tanh(preact[:, :PAIR])
    opened = 0.5 * jnp.tanh(0.5 * preact[:, PAIR:]) + 0.5
    return filtered, opened


def pairs(columns):
    return [slice(at, at + PAIR) for at in range(0, columns, PAIR)]


def wides(columns):
    return [slice(2 * at, 2 * at + 2 * PAIR) for at in range(0, columns, PAIR)]


def send_kernel(
    rows_hbm,
    series_hbm,
    mix_hbm,
    cot_hbm,
    count_hbm,
    values_hbm,
    out_hbm,
    rows_ref,
    series_ref,
    mix_ref,
    cot_ref,
    count_ref,
    values_ref,
    out_ref,
    came,
    gone,
):
    nodes, columns = series_ref.shape
    _, groups, cap, _ = out_ref.shape
    slots = groups * cap
    brought = [
        pltpu.make_async_copy(source, target, came.at[n])
        for n, (source, target) in enumerate(
            [
                (rows_hbm, rows_ref),
                (series_hbm, series_ref),
                (mix_hbm, mix_ref),
                (cot_hbm, cot_ref),
                (count_hbm, count_ref),
                (values_hbm, values_ref),
            ]
        )
    ]
    for copy in brought:
        copy.start()
    sent = [
        pltpu.make_async_copy(out_ref.at[n], out_hbm.at[:, pl.ds(n * cap, cap), :], gone.at[n])
        for n in range(2)
    ]
    for copy in brought:
        copy.wait()
    pick = picker(rows_ref, nodes, slots)
    live = live_values(values_ref, count_ref)
    mix = two_steps(mix_ref[...])[:, PAIR:]
    mixed_grad = jnp.concatenate([dot(cot_ref[:, c], mix).astype(BF16) for c in pairs(columns)], axis=1)
    listed = dot_tn(pick, series_ref[...]).astype(BF16)
    out_ref[0] = to_order(listed.reshape(groups, cap, columns))
    sent[0].start()
    returned = dot_tn(live, mixed_grad).astype(BF16)
    out_ref[1] = to_order(returned.reshape(groups, cap, columns))
    sent[1].start()
    sent[0].wait()
    sent[1].wait()


def local_grad_kernel(
    cot_ref,
    mix_ref,
    local_ref,
    rows_ref,
    values_ref,
    count_ref,
    blocks_ref,
    out_ref,
    slots_ref,
):
    nodes, slots = values_ref.shape
    slots_ref[:, :slots] = picker(rows_ref, nodes, slots)
    slots_ref[:, slots:] = live_values(values_ref, count_ref)
    mix = two_steps(mix_ref[...])
    tiles, per_tile, size, _ = local_ref.shape
    kept = []
    for c in pairs(cot_ref.shape[1]):
        grads = dot(cot_ref[:, c], mix)
        out_ref[:, c] = grads[:, :PAIR]
        kept.append(grads[:, PAIR:].astype(BF16))
    mixed_grad = jnp.concatenate(kept, axis=1)
    for t in range(tiles):
        for b in range(per_tile):
            rows = pl.ds(pl.multiple_of(blocks_ref[t, b] * size, size), size)
            out_ref[rows, :] += dot_tn(local_ref[t, b], mixed_grad[t * size : (t + 1) * size])


def own_kernel(
    series_ref,
    delayed_ref,
    conv_ref,
    bias_ref,
    mix_ref,
    local_ref,
    blocks_ref,
    base_ref,
    slope_ref,
    weight_ref,
    hidden_ref,
):
    weight = conv_pair(conv_ref)
    bias = bias_pair(bias_ref)
    mix = two_steps(mix_ref[...])
    weight_ref[: 2 * PAIR] = weight
    weight_ref[2 * PAIR :] = mix
    tiles, per_tile, size, _ = local_ref.shape
    columns = series_ref.shape[1]
    for c, w in zip(pairs(columns), wides(columns)):
        stacked = jnp.concatenate([delayed_ref[:, c], series_ref[:, c]], axis=1)
        filtered, opened = tanh_sigmoid(dot(stacked, weight) + bias)
        hidden_ref[:, c] = (filtered * opened).astype(BF16)
        first = opened * (1.0 - filtered * filtered)
        second = filtered * opened * (1.0 - opened)
        slope_ref[:, w] = jnp.concatenate([first, second], axis=1)
    sums = []
    for t in range(tiles):
        total = None
        for b in range(per_tile):
            rows = pl.ds(pl.multiple_of(blocks_ref[t, b] * size, size), size)
            term = dot(local_ref[t, b], hidden_ref[rows, :])
            total = term if total is None else total + term
        sums.append(total.astype(BF16))
    local_sum = jnp.concatenate(sums, axis=0)
    for c in pairs(columns):
        both = jnp.concatenate([hidden_ref[:, c], local_sum[:, c]], axis=1)
        base_ref[:, c] = series_ref[:, c].astype(F32) + dot_nt(both, mix)


def gate_grad_kernel(got_ref, partial_ref, slope_ref, slots_ref, weight_ref, gate_ref, swap_ref):
    groups, both, columns = got_ref.shape
    cap = both // 2
    second_half = lax.axis_index("tm") >= lax.axis_size("tm") // 2
    back = from_order(got_ref[:, cap:, :]).reshape(groups * cap, columns)
    upstream = (partial_ref[...] + dot(slots_ref[:, : groups * cap], back)).astype(BF16).astype(F32)
    for c, w in zip(pairs(columns), wides(columns)):
        up = upstream[:, c]
        gate_ref[:, w] = (jnp.concatenate([up, up], axis=1) * slope_ref[:, w]).astype(BF16)

    @pl.when(second_half)
    def _():
        for c, w in zip(pairs(columns), wides(columns)):
            swap_ref[:, c] = dot_nt(gate_ref[:, w], weight_ref[:PAIR]).astype(BF16)

    @pl.when(jnp.logical_not(second_half))
    def _():
        swap_ref[...] = from_order(got_ref[:, :cap, :]).reshape(groups * cap, columns)


def last_kernel(
    came_ref,
    got_ref,
    gate_ref,
    slots_ref,
    base_ref,
    cot_ref,
    weight_ref,
    bias_ref,
    out_hbm,
    grad_hbm,
    out_ref,
    grad_ref,
    gone,
):
    groups, both, columns = got_ref.shape
    cap = both // 2
    slots = groups * cap
    nodes = cot_ref.shape[0]
    second_half = lax.axis_index("tm") >= lax.axis_size("tm") // 2
    came = came_ref[jnp.where(second_half, 0, 1)].astype(F32)
    before = jnp.where(second_half, came, 0.0).astype(BF16)
    listed = from_order(got_ref[:, :cap, :]).reshape(slots, columns)
    bias = bias_pair(bias_ref)
    kept = []
    for c in pairs(columns):
        stacked = jnp.concatenate([before[:, c], listed[:, c]], axis=1)
        filtered, opened = tanh_sigmoid(dot(stacked, weight_ref[: 2 * PAIR]) + bias)
        kept.append((filtered * opened).astype(BF16))
    hidden = jnp.concatenate(kept, axis=1)
    mixed = dot(slots_ref[:, slots:], hidden).astype(BF16)
    for c in pairs(columns):
        added = dot_nt(mixed[:, c], weight_ref[2 * PAIR :, PAIR:])
        out_ref[:, c] = (base_ref[:, c] + added).astype(BF16)
    out_copy = pltpu.make_async_copy(out_ref, out_hbm, gone.at[0])
    out_copy.start()
    later = jnp.where(second_half, 0.0, came)
    for c, w in zip(pairs(columns), wides(columns)):
        grad = (dot_nt(gate_ref[:, w], weight_ref[PAIR : 2 * PAIR]) + later[:, c]).astype(BF16)
        grad_ref[:, c] = (cot_ref[:, c].astype(F32) + grad.astype(F32)).astype(BF16)
    grad_copy = pltpu.make_async_copy(grad_ref, grad_hbm, gone.at[1])
    grad_copy.start()
    out_copy.wait()
    grad_copy.wait()


VMEM = pl.BlockSpec(memory_space=pltpu.VMEM)
SMEM = pl.BlockSpec(memory_space=pltpu.SMEM)
HBM = pl.BlockSpec(memory_space=pltpu.HBM)


def call(kernel, outs, *args, scalars=(), ins=VMEM, out=VMEM, scratch=(), limit=32):
    many = isinstance(outs, tuple)
    return pl.pallas_call(
        kernel,
        out_shape=outs,
        in_specs=[SMEM if n in scalars else ins for n in range(len(args))],
        out_specs=tuple(out for _ in outs) if many else out,
        scratch_shapes=scratch,
        compiler_params=pltpu.CompilerParams(vmem_limit_bytes=limit << 20),
        cost_estimate=pl.CostEstimate(flops=1 << 27, bytes_accessed=1 << 21, transcendentals=0),
    )(*args)


def local(
    series,
    conv_weight,
    conv_bias,
    mix_weight,
    local_blocks,
    local_values,
    send_rows,
    send_count,
    remote_values,
    cotangent,
):
    nodes, columns = series.shape
    groups, cap = send_rows.shape[1:]
    slots = groups * cap
    places = lax.axis_size("tm")
    half = places // 2

    def shape(rows, cols, kind):
        return jax.ShapeDtypeStruct((rows, cols), kind)

    mix = mix_weight.T
    bias = conv_bias.reshape(1, -1)
    first = (send_rows, series, mix, cotangent, send_count, remote_values)
    send = call(
        send_kernel,
        jax.ShapeDtypeStruct((groups, 2 * cap, columns), BF16),
        *first,
        ins=HBM,
        out=HBM,
        limit=60,
        scratch=[pltpu.VMEM(a.shape, a.dtype) for a in first]
        + [
            pltpu.VMEM((2, groups, cap, columns), BF16),
            pltpu.SemaphoreType.DMA((len(first),)),
            pltpu.SemaphoreType.DMA((2,)),
        ],
    )
    got = lax.all_to_all(send, "node", 0, 0, axis_index_groups=[list(ORDER)], tiled=True)
    delayed = lax.ppermute(series, "tm", [(i, i + half) for i in range(half)])
    partial, picked_live = call(
        local_grad_kernel,
        (shape(nodes, columns, F32), shape(nodes, 2 * slots, BF16)),
        cotangent,
        mix,
        local_values,
        send_rows,
        remote_values,
        send_count,
        local_blocks,
        scalars=(6,),
    )
    base, slope, weight = call(
        own_kernel,
        (shape(nodes, columns, F32), shape(nodes, 2 * columns, F32), shape(3 * PAIR, 2 * PAIR, BF16)),
        series,
        delayed,
        conv_weight,
        bias,
        mix,
        local_values,
        local_blocks,
        scalars=(6,),
        scratch=[pltpu.VMEM((nodes, columns), BF16)],
    )
    gate, swap = call(
        gate_grad_kernel,
        (shape(nodes, 2 * columns, BF16), shape(nodes, columns, BF16)),
        got,
        partial,
        slope,
        picked_live,
        weight,
    )
    came = lax.all_gather(swap, "tm", axis_index_groups=[[i, i + half] for i in range(half)])
    return call(
        last_kernel,
        (shape(nodes, columns, BF16), shape(nodes, columns, BF16)),
        came,
        got,
        gate,
        picked_live,
        base,
        cotangent,
        weight,
        bias,
        out=HBM,
        scratch=[
            pltpu.VMEM((nodes, columns), BF16),
            pltpu.VMEM((nodes, columns), BF16),
            pltpu.SemaphoreType.DMA((2,)),
        ],
    )


def solution(mesh):
    in_specs = (
        P("node", "tm"),
        P(),
        P(),
        P(),
        P("node", None),
        P("node", None, None, None),
        P("node", None, None),
        P(),
        P("node", None),
        P("node", "tm"),
    )
    out_specs = (P("node", "tm"), P("node", "tm"))
    return jax.shard_map(local, mesh=mesh, in_specs=in_specs, out_specs=out_specs, check_vma=False)
```

```python
import jax
import jax.numpy as jnp
from jax import lax
from jax.experimental import pallas as pl
from jax.experimental.pallas import tpu as pltpu
from jax.sharding import PartitionSpec as P

C = 64
PAIR = 2 * C
F32 = jnp.float32
BF16 = jnp.bfloat16
ORDER = (11, 12, 6, 13, 9, 14, 8, 15, 7, 0, 10, 1, 5, 2, 4, 3)


def dot(a, b):
    return lax.dot_general(a, b, (((1,), (0,)), ((), ())), preferred_element_type=F32)


def dot_nt(a, b):
    return lax.dot_general(a, b, (((1,), (1,)), ((), ())), preferred_element_type=F32)


def dot_tn(a, b):
    return lax.dot_general(a, b, (((0,), (0,)), ((), ())), preferred_element_type=F32)


def iota(shape, dim):
    return lax.broadcasted_iota(jnp.int32, shape, dim)


def two_steps(weight):
    weight = weight.astype(F32)
    turned = pltpu.roll(weight, C, 1)
    low = iota(weight.shape, 1) < C
    even = jnp.concatenate([jnp.where(low, weight, 0.0), jnp.where(low, turned, 0.0)], axis=1)
    odd = jnp.concatenate([jnp.where(low, 0.0, turned), jnp.where(low, 0.0, weight)], axis=1)
    return jnp.concatenate([even, odd], axis=0).astype(BF16)


def conv_pair(conv_ref):
    return jnp.concatenate([two_steps(conv_ref[:C]), two_steps(conv_ref[C:])], axis=0)


def bias_pair(bias_ref):
    bias = bias_ref[...]
    turned = pltpu.roll(jnp.broadcast_to(bias, (8, PAIR)), C, 1)[:1]
    low = iota(bias.shape, 1) < C
    return jnp.concatenate([jnp.where(low, bias, turned), jnp.where(low, turned, bias)], axis=1)


def spread(table, slots):
    groups, cap = table.shape
    spot = iota((cap, slots), 1)
    place = jnp.where(lax.rem(spot, cap) == iota((cap, slots), 0), 1.0, 0.0).astype(BF16)
    wide = dot(table.astype(F32).astype(BF16), place)
    mine = iota((groups, slots), 1) // cap == iota((groups, slots), 0)
    return jnp.sum(jnp.where(mine, wide, 0.0), axis=0, keepdims=True)


def picker(rows_ref, nodes, slots):
    rows = spread(rows_ref[0], slots)
    return jnp.where(iota((nodes, slots), 0).astype(F32) == rows, 1.0, 0.0).astype(BF16)


def live_values(values_ref, count_ref):
    groups = count_ref.shape[0]
    slots = values_ref.shape[1]
    cap = slots // groups
    me = lax.axis_index("node")
    counts = count_ref[...].astype(F32)
    counts = jnp.where(iota(counts.shape, 1) == me, counts, 0.0)
    counts = jnp.sum(counts, axis=1, keepdims=True)
    column = iota((groups, slots), 1)
    mine = column // cap == iota((groups, slots), 0)
    limit = jnp.sum(jnp.where(mine, counts, 0.0), axis=0, keepdims=True)
    alive = lax.rem(column, cap)[:1].astype(F32) < limit
    return jnp.where(alive, values_ref[...].astype(F32), 0.0).astype(BF16)


def to_order(blocks):
    return jnp.concatenate([blocks[q : q + 1] for q in ORDER], axis=0)


def from_order(blocks):
    places = [ORDER.index(q) for q in range(len(ORDER))]
    return jnp.concatenate([blocks[k : k + 1] for k in places], axis=0)


def tanh_sigmoid(preact):
    filtered = jnp.tanh(preact[:, :PAIR])
    opened = 0.5 * jnp.tanh(0.5 * preact[:, PAIR:]) + 0.5
    return filtered, opened


def pairs(columns):
    return [slice(at, at + PAIR) for at in range(0, columns, PAIR)]


def wides(columns):
    return [slice(2 * at, 2 * at + 2 * PAIR) for at in range(0, columns, PAIR)]


def send_kernel(
    rows_hbm,
    series_hbm,
    mix_hbm,
    cot_hbm,
    count_hbm,
    values_hbm,
    out_hbm,
    rows_ref,
    series_ref,
    mix_ref,
    cot_ref,
    count_ref,
    values_ref,
    out_ref,
    came,
    gone,
):
    nodes, columns = series_ref.shape
    _, groups, cap, _ = out_ref.shape
    slots = groups * cap
    brought = [
        pltpu.make_async_copy(source, target, came.at[n])
        for n, (source, target) in enumerate(
            [
                (rows_hbm, rows_ref),
                (series_hbm, series_ref),
                (mix_hbm, mix_ref),
                (cot_hbm, cot_ref),
                (count_hbm, count_ref),
                (values_hbm, values_ref),
            ]
        )
    ]
    for copy in brought:
        copy.start()
    sent = [
        pltpu.make_async_copy(out_ref.at[n], out_hbm.at[:, pl.ds(n * cap, cap), :], gone.at[n])
        for n in range(2)
    ]
    for n in (0, 4, 2):
        brought[n].wait()
    mix = two_steps(mix_ref[...])[:, PAIR:]
    pick = picker(rows_ref, nodes, slots)
    for n in (1, 3, 5):
        brought[n].wait()
    live = live_values(values_ref, count_ref)
    mixed_grad = jnp.concatenate([dot(cot_ref[:, c], mix).astype(BF16) for c in pairs(columns)], axis=1)
    listed = dot_tn(pick, series_ref[...]).astype(BF16)
    out_ref[0] = to_order(listed.reshape(groups, cap, columns))
    sent[0].start()
    returned = dot_tn(live, mixed_grad).astype(BF16)
    out_ref[1] = to_order(returned.reshape(groups, cap, columns))
    sent[1].start()
    sent[0].wait()
    sent[1].wait()


def local_grad_kernel(
    cot_ref,
    mix_ref,
    local_ref,
    rows_ref,
    values_ref,
    count_ref,
    blocks_ref,
    out_ref,
    slots_ref,
):
    nodes, slots = values_ref.shape
    slots_ref[:, :slots] = picker(rows_ref, nodes, slots)
    slots_ref[:, slots:] = live_values(values_ref, count_ref)
    mix = two_steps(mix_ref[...])
    tiles, per_tile, size, _ = local_ref.shape
    kept = []
    for c in pairs(cot_ref.shape[1]):
        grads = dot(cot_ref[:, c], mix)
        out_ref[:, c] = grads[:, :PAIR]
        kept.append(grads[:, PAIR:].astype(BF16))
    mixed_grad = jnp.concatenate(kept, axis=1)
    for t in range(tiles):
        for b in range(per_tile):
            rows = pl.ds(pl.multiple_of(blocks_ref[t, b] * size, size), size)
            out_ref[rows, :] += dot_tn(local_ref[t, b], mixed_grad[t * size : (t + 1) * size])


def own_kernel(
    series_ref,
    delayed_ref,
    conv_ref,
    bias_ref,
    mix_ref,
    local_ref,
    blocks_ref,
    base_ref,
    slope_ref,
    weight_ref,
    hidden_ref,
):
    weight = conv_pair(conv_ref)
    bias = bias_pair(bias_ref)
    mix = two_steps(mix_ref[...])
    weight_ref[: 2 * PAIR] = weight
    weight_ref[2 * PAIR :] = mix
    tiles, per_tile, size, _ = local_ref.shape
    columns = series_ref.shape[1]
    for c, w in zip(pairs(columns), wides(columns)):
        stacked = jnp.concatenate([delayed_ref[:, c], series_ref[:, c]], axis=1)
        filtered, opened = tanh_sigmoid(dot(stacked, weight) + bias)
        hidden_ref[:, c] = (filtered * opened).astype(BF16)
        first = opened * (1.0 - filtered * filtered)
        second = filtered * opened * (1.0 - opened)
        slope_ref[:, w] = jnp.concatenate([first, second], axis=1)
    sums = []
    for t in range(tiles):
        total = None
        for b in range(per_tile):
            rows = pl.ds(pl.multiple_of(blocks_ref[t, b] * size, size), size)
            term = dot(local_ref[t, b], hidden_ref[rows, :])
            total = term if total is None else total + term
        sums.append(total.astype(BF16))
    local_sum = jnp.concatenate(sums, axis=0)
    for c in pairs(columns):
        both = jnp.concatenate([hidden_ref[:, c], local_sum[:, c]], axis=1)
        base_ref[:, c] = series_ref[:, c].astype(F32) + dot_nt(both, mix)


def gate_grad_kernel(got_ref, partial_ref, slope_ref, slots_ref, weight_ref, gate_ref, swap_ref):
    groups, both, columns = got_ref.shape
    cap = both // 2
    second_half = lax.axis_index("tm") >= lax.axis_size("tm") // 2
    back = from_order(got_ref[:, cap:, :]).reshape(groups * cap, columns)
    upstream = (partial_ref[...] + dot(slots_ref[:, : groups * cap], back)).astype(BF16).astype(F32)
    for c, w in zip(pairs(columns), wides(columns)):
        up = upstream[:, c]
        gate_ref[:, w] = (jnp.concatenate([up, up], axis=1) * slope_ref[:, w]).astype(BF16)

    @pl.when(second_half)
    def _():
        for c, w in zip(pairs(columns), wides(columns)):
            swap_ref[:, c] = dot_nt(gate_ref[:, w], weight_ref[:PAIR]).astype(BF16)

    @pl.when(jnp.logical_not(second_half))
    def _():
        swap_ref[...] = from_order(got_ref[:, :cap, :]).reshape(groups * cap, columns)


def last_kernel(
    came_ref,
    got_ref,
    gate_ref,
    slots_ref,
    base_ref,
    cot_ref,
    weight_ref,
    bias_ref,
    out_hbm,
    grad_hbm,
    out_ref,
    grad_ref,
    gone,
):
    groups, both, columns = got_ref.shape
    cap = both // 2
    slots = groups * cap
    nodes = cot_ref.shape[0]
    second_half = lax.axis_index("tm") >= lax.axis_size("tm") // 2
    came = came_ref[jnp.where(second_half, 0, 1)].astype(F32)
    before = jnp.where(second_half, came, 0.0).astype(BF16)
    listed = from_order(got_ref[:, :cap, :]).reshape(slots, columns)
    bias = bias_pair(bias_ref)
    kept = []
    for c in pairs(columns):
        stacked = jnp.concatenate([before[:, c], listed[:, c]], axis=1)
        filtered, opened = tanh_sigmoid(dot(stacked, weight_ref[: 2 * PAIR]) + bias)
        kept.append((filtered * opened).astype(BF16))
    hidden = jnp.concatenate(kept, axis=1)
    mixed = dot(slots_ref[:, slots:], hidden).astype(BF16)
    for c in pairs(columns):
        added = dot_nt(mixed[:, c], weight_ref[2 * PAIR :, PAIR:])
        out_ref[:, c] = (base_ref[:, c] + added).astype(BF16)
    out_copy = pltpu.make_async_copy(out_ref, out_hbm, gone.at[0])
    out_copy.start()
    later = jnp.where(second_half, 0.0, came)
    for c, w in zip(pairs(columns), wides(columns)):
        grad = (dot_nt(gate_ref[:, w], weight_ref[PAIR : 2 * PAIR]) + later[:, c]).astype(BF16)
        grad_ref[:, c] = (cot_ref[:, c].astype(F32) + grad.astype(F32)).astype(BF16)
    grad_copy = pltpu.make_async_copy(grad_ref, grad_hbm, gone.at[1])
    grad_copy.start()
    out_copy.wait()
    grad_copy.wait()


VMEM = pl.BlockSpec(memory_space=pltpu.VMEM)
SMEM = pl.BlockSpec(memory_space=pltpu.SMEM)
HBM = pl.BlockSpec(memory_space=pltpu.HBM)


def call(kernel, outs, *args, scalars=(), ins=VMEM, out=VMEM, scratch=(), limit=32):
    many = isinstance(outs, tuple)
    return pl.pallas_call(
        kernel,
        out_shape=outs,
        in_specs=[SMEM if n in scalars else ins for n in range(len(args))],
        out_specs=tuple(out for _ in outs) if many else out,
        scratch_shapes=scratch,
        compiler_params=pltpu.CompilerParams(vmem_limit_bytes=limit << 20),
        cost_estimate=pl.CostEstimate(flops=1 << 27, bytes_accessed=1 << 21, transcendentals=0),
    )(*args)


def local(
    series,
    conv_weight,
    conv_bias,
    mix_weight,
    local_blocks,
    local_values,
    send_rows,
    send_count,
    remote_values,
    cotangent,
):
    nodes, columns = series.shape
    groups, cap = send_rows.shape[1:]
    slots = groups * cap
    places = lax.axis_size("tm")
    half = places // 2

    def shape(rows, cols, kind):
        return jax.ShapeDtypeStruct((rows, cols), kind)

    mix = mix_weight.T
    bias = conv_bias.reshape(1, -1)
    first = (send_rows, series, mix, cotangent, send_count, remote_values)
    send = call(
        send_kernel,
        jax.ShapeDtypeStruct((groups, 2 * cap, columns), BF16),
        *first,
        ins=HBM,
        out=HBM,
        limit=60,
        scratch=[pltpu.VMEM(a.shape, a.dtype) for a in first]
        + [
            pltpu.VMEM((2, groups, cap, columns), BF16),
            pltpu.SemaphoreType.DMA((len(first),)),
            pltpu.SemaphoreType.DMA((2,)),
        ],
    )
    got = lax.all_to_all(send, "node", 0, 0, axis_index_groups=[list(ORDER)], tiled=True)
    delayed = lax.ppermute(series, "tm", [(i, i + half) for i in range(half)])
    partial, picked_live = call(
        local_grad_kernel,
        (shape(nodes, columns, F32), shape(nodes, 2 * slots, BF16)),
        cotangent,
        mix,
        local_values,
        send_rows,
        remote_values,
        send_count,
        local_blocks,
        scalars=(6,),
    )
    base, slope, weight = call(
        own_kernel,
        (shape(nodes, columns, F32), shape(nodes, 2 * columns, F32), shape(3 * PAIR, 2 * PAIR, BF16)),
        series,
        delayed,
        conv_weight,
        bias,
        mix,
        local_values,
        local_blocks,
        scalars=(6,),
        scratch=[pltpu.VMEM((nodes, columns), BF16)],
    )
    gate, swap = call(
        gate_grad_kernel,
        (shape(nodes, 2 * columns, BF16), shape(nodes, columns, BF16)),
        got,
        partial,
        slope,
        picked_live,
        weight,
    )
    came = lax.all_gather(swap, "tm", axis_index_groups=[[i, i + half] for i in range(half)])
    return call(
        last_kernel,
        (shape(nodes, columns, BF16), shape(nodes, columns, BF16)),
        came,
        got,
        gate,
        picked_live,
        base,
        cotangent,
        weight,
        bias,
        out=HBM,
        scratch=[
            pltpu.VMEM((nodes, columns), BF16),
            pltpu.VMEM((nodes, columns), BF16),
            pltpu.SemaphoreType.DMA((2,)),
        ],
    )


def solution(mesh):
    in_specs = (
        P("node", "tm"),
        P(),
        P(),
        P(),
        P("node", None),
        P("node", None, None, None),
        P("node", None, None),
        P(),
        P("node", None),
        P("node", "tm"),
    )
    out_specs = (P("node", "tm"), P("node", "tm"))
    return jax.shard_map(local, mesh=mesh, in_specs=in_specs, out_specs=out_specs, check_vma=False)
```
